32 devices in a mesh: frame: 2 (over y), row: 4 (over x, core), fsdp: 4 (over z).
Axes of the slice: x: 2, y: 2, z: 4, core: 2. Of those that a mesh axis runs over, the one named last changes fastest.
Arguments:
- query: bfloat16 [4, 16, 48, 2560], P('frame', 'row', 'fsdp'), may hold values from -20 to 20
- key_value: bfloat16 [2, 4, 16, 48, 2560], P(None, 'frame', 'row', 'fsdp'), may hold values from -6 to 6
- out_weight: bfloat16 [2560, 2560], P(None, 'fsdp'), may hold values from -0.125 to 0.125
- mod_table: float32 [16, 2560], replicated, may hold values from -4 to 4
- step: int32 [1], replicated, may hold values from 0 to 15
- window: int32 [20, 3], replicated, may hold values from 0 to 2, as said below
Outputs:
- mixed: bfloat16 [4, 16, 48, 2560], P('frame', 'row', 'fsdp')
The draws below stay inside these ranges and needn't reach their ends.
Inputs may be any that keep to these rules, and one draw needn't show every extreme that they name: `window`: Half-extents along frames are at most 1, along rows at most 2, along columns at most 2; every head has a nonzero half-extent along some dimension; some head has exactly 1, 2 and 2, and some head has 0 along frames.
All inputs are finite; a program needn't handle non-finite values.
Results may differ from the reference program's by a relative error of at most 0.0057.
Values may be sent and summed in bfloat16 or wider, within the bound.
A program may use at most 128 MiB of HBM per device.

```python
import math
import jax
import jax.numpy as jnp
from jax import lax

HEADS = 20
HEAD_DIM = 128
D_OUT = 2560
STEPS = 16
WF = 1
WR = 2
WC = 2
QW = 2560
NF = 4
NR = 16
NC = 48


def draw_query(key, part):
    noise = jnp.clip(jax.random.normal(jax.random.fold_in(key, 1), (NF, NR, NC, HEADS * HEAD_DIM), jnp.float32), -6.0, 6.0)
    return noise.astype(jnp.bfloat16)


def draw_key_value(key, part):
    noise = jnp.clip(jax.random.normal(jax.random.fold_in(key, 2), (2, NF, NR, NC, HEADS * HEAD_DIM), jnp.float32), -6.0, 6.0)
    return noise.astype(jnp.bfloat16)


def draw_window(key, part):
    bounds = jnp.array([WF + 1, WR + 1, WC + 1], jnp.int32)
    base = jax.random.randint(jax.random.fold_in(key, 3), (HEADS, 3), 0, bounds[None, :])
    full_head = jax.random.randint(jax.random.fold_in(key, 4), (), 0, HEADS)
    other_head = (full_head + 1 + jax.random.randint(jax.random.fold_in(key, 5), (), 0, HEADS - 1)) % HEADS
    heads_iota = jnp.arange(HEADS)
    base = jnp.where((heads_iota == full_head)[:, None], jnp.array([WF, WR, WC], jnp.int32)[None, :], base)
    base = jnp.where((heads_iota == other_head)[:, None], jnp.array([0, WR, WC], jnp.int32)[None, :], base)
    empty_rows = jnp.sum(base, axis=1) == 0
    base = base.at[:, 2].set(jnp.where(empty_rows, WC, base[:, 2]))
    return base.astype(jnp.int32)


def block_scale(key, shape, cuts, low, high):
    level, own = 1.0, jax.random.fold_in(key, 6)
    for axis_at, blocks in cuts:
        draws = jnp.exp(jax.random.uniform(jax.random.fold_in(own, axis_at), (blocks,), jnp.float32, low / len(cuts), high / len(cuts)))
        level = level * jnp.repeat(draws, shape[axis_at] // blocks).reshape([-1 if axis == axis_at else 1 for axis in range(len(shape))])
    return level


def gaussian(rng, shape, scale, limit, cuts=(), held_as=jnp.bfloat16):
    level = block_scale(rng, shape, cuts, -0.22, 0.18) if cuts else 1.0
    values = jax.random.normal(rng, shape, jnp.float32) * scale * level
    return jnp.minimum(jnp.maximum(values, -limit), limit).astype(held_as)


def setup_inputs(seed: int = 0) -> dict:
    key_of = jax.random.split(jax.random.key(seed), 7)
    query = draw_query(jax.random.fold_in(key_of[6], 71), 0)
    key_value = draw_key_value(jax.random.fold_in(key_of[6], 71), 0)
    out_weight = gaussian(key_of[2], (QW, D_OUT), QW ** -0.5, 0.125, ((1, 4),))
    mod_table = gaussian(key_of[3], (STEPS, D_OUT), 1.0, 4.0, (), jnp.float32)
    step = jax.random.randint(key_of[4], (1,), 0, STEPS).astype(jnp.int32)
    window = draw_window(jax.random.fold_in(key_of[6], 71), 0)
    return {"query": query, "key_value": key_value, "out_weight": out_weight, "mod_table": mod_table, "step": step, "window": window}


def reference(query, key_value, out_weight, mod_table, step, window):
    frame_count, row_count, column_count, feature_width = query.shape
    head_count = feature_width // HEAD_DIM
    score_scale = 1.0 / math.sqrt(HEAD_DIM)
    queries = query.astype(jnp.float32).reshape(frame_count, row_count, column_count, head_count, HEAD_DIM)
    pairs = key_value.astype(jnp.float32).reshape(2, frame_count, row_count, column_count, head_count, HEAD_DIM)
    padded = jnp.pad(pairs, ((0, 0), (WF, WF), (WR, WR), (WC, WC), (0, 0), (0, 0)))
    frame_pos = jnp.arange(frame_count)
    row_pos = jnp.arange(row_count)
    column_pos = jnp.arange(column_count)
    shifts = [(sf, sr, sc) for sf in range(-WF, WF + 1) for sr in range(-WR, WR + 1) for sc in range(-WC, WC + 1)]
    score_list = []
    for sf, sr, sc in shifts:
        moved = padded[0, WF + sf:WF + sf + frame_count, WR + sr:WR + sr + row_count, WC + sc:WC + sc + column_count]
        values_here = lax.optimization_barrier(jnp.sum(queries * moved, axis=-1)) * score_scale
        inside_f = (frame_pos + sf >= 0) & (frame_pos + sf < frame_count)
        inside_r = (row_pos + sr >= 0) & (row_pos + sr < row_count)
        inside_c = (column_pos + sc >= 0) & (column_pos + sc < column_count)
        inside = inside_f[:, None, None] & inside_r[None, :, None] & inside_c[None, None, :]
        allowed = (abs(sf) <= window[:, 0]) & (abs(sr) <= window[:, 1]) & (abs(sc) <= window[:, 2])
        usable = inside[..., None] & allowed[None, None, None, :]
        score_list.append(jnp.where(usable, values_here, jnp.float32(-1e+30)))
    stacked = jnp.stack(score_list)
    highest = lax.optimization_barrier(jnp.max(stacked, axis=0))
    exponent = jnp.exp(stacked - highest)
    denominator = lax.optimization_barrier(jnp.sum(exponent, axis=0))
    weights = (exponent / denominator).astype(jnp.bfloat16)
    weights = lax.optimization_barrier(weights).astype(jnp.float32)
    accum = jnp.zeros((frame_count, row_count, column_count, head_count, HEAD_DIM), jnp.float32)
    for index, (sf, sr, sc) in enumerate(shifts):
        moved = padded[1, WF + sf:WF + sf + frame_count, WR + sr:WR + sr + row_count, WC + sc:WC + sc + column_count]
        accum = accum + weights[index][..., None] * moved
    attn = accum.astype(jnp.bfloat16).reshape(frame_count * row_count * column_count, feature_width)
    gate = lax.dynamic_slice_in_dim(mod_table, step[0].astype(jnp.int32), 1, 0)[0]
    product = jnp.dot(attn, out_weight, preferred_element_type=jnp.float32)
    mixed = (product * gate).astype(jnp.bfloat16)
    return mixed.reshape(frame_count, row_count, column_count, -1)
```

```python
import functools
import math

import jax
import jax.numpy as jnp
from jax import lax
from jax.experimental import pallas as pl
from jax.experimental.pallas import tpu as pltpu
from jax.sharding import PartitionSpec as P

HEAD_DIM = 128
QUARTERS = 4
MESH = pl.DeviceIdType.MESH


def kernel(
    sizes, gin, q_ref, w_hbm, gate_ref, win_ref, out_ref,
    grid, bias, attn, w_ref, y_out, y_in,
    halo_send, halo_recv, attn_send, attn_recv, y_send, y_recv, local_sem,
):
    n_frame, n_row, n_col = sizes
    slots = grid.shape[0]
    groups = attn.shape[0]
    tokens = attn.shape[2]
    own_frames, own_rps, own_cps = gin.shape[:3]
    me_f = lax.axis_index("frame")
    me_r = lax.axis_index("row")
    me_c = lax.axis_index("fsdp")

    w_copy = pltpu.make_async_copy(w_hbm, w_ref, local_sem.at[0])
    w_copy.start()
    own_copy = pltpu.make_async_copy(
        gin, grid.at[pl.ds(0, own_frames), pl.ds(0, own_rps), pl.ds(0, own_cps)], local_sem.at[1]
    )
    own_copy.start()

    barrier = pltpu.get_barrier_semaphore()

    def neighbours(axis, me, count):
        return ((axis, me + 1, me < count - 1), (axis, me - 1, me > 0))

    near = neighbours("frame", me_f, n_frame) + neighbours("row", me_r, n_row)
    for axis, other, there in near:
        @pl.when(there)
        def _():
            pl.semaphore_signal(barrier, inc=1, device_id={axis: other}, device_id_type=MESH)

    def greet(k, carry):
        peer = lax.rem(me_c + k, n_col)
        pl.semaphore_signal(barrier, inc=1, device_id={"fsdp": peer}, device_id_type=MESH)
        return carry

    lax.fori_loop(1, n_col, greet, 0)
    greetings = n_col - 1
    for _, _, there in near:
        greetings += there.astype(jnp.int32)
    pl.semaphore_wait(barrier, greetings)

    def copy(src, dst, index, axis, other):
        return pltpu.make_async_remote_copy(
            src_ref=src, dst_ref=dst, send_sem=halo_send.at[index], recv_sem=halo_recv.at[index],
            device_id={axis: other}, device_id_type=MESH,
        )

    own_f = pl.ds(0, own_frames)
    halo_f = pl.ds(own_frames, slots - own_frames)
    own_r = pl.ds(0, own_rps)
    halo_r = pl.ds(own_rps, 2)
    own_c = pl.ds(0, own_cps)
    below, above = own_rps, own_rps + 1
    left, right = own_cps, own_cps + 1
    low_slot, high_slot = own_frames, slots - 1
    steps = {}

    def add(name, axis, me, count, index, up, down):
        steps[name] = (
            (copy(up[0], up[1], index, axis, me + 1), me < count - 1, me > 0),
            (copy(down[0], down[1], index + 1, axis, me - 1), me > 0, me < count - 1),
        )

    add("f", "frame", me_f, n_frame, 0,
        (gin.at[own_frames - 1], grid.at[low_slot, own_r, own_c]),
        (gin.at[0], grid.at[high_slot, own_r, own_c]))
    add("r1", "row", me_r, n_row, 2,
        (gin.at[:, own_rps - 1], grid.at[own_f, below, own_c]),
        (gin.at[:, 0], grid.at[own_f, above, own_c]))
    add("r2", "row", me_r, n_row, 4,
        (grid.at[halo_f, own_rps - 1, own_c], grid.at[halo_f, below, own_c]),
        (grid.at[halo_f, 0, own_c], grid.at[halo_f, above, own_c]))
    add("c1", "fsdp", me_c, n_col, 6,
        (gin.at[:, :, own_cps - 1], grid.at[own_f, own_r, left]),
        (gin.at[:, :, 0], grid.at[own_f, own_r, right]))
    add("c2", "fsdp", me_c, n_col, 8,
        (grid.at[own_f, halo_r, own_cps - 1], grid.at[own_f, halo_r, left]),
        (grid.at[own_f, halo_r, 0], grid.at[own_f, halo_r, right]))
    all_r = pl.ds(0, own_rps + 2)
    add("c3", "fsdp", me_c, n_col, 10,
        (grid.at[halo_f, all_r, own_cps - 1], grid.at[halo_f, all_r, left]),
        (grid.at[halo_f, all_r, 0], grid.at[halo_f, all_r, right]))

    def start(name):
        for step, sends, _ in steps[name]:
            @pl.when(sends)
            def _():
                step.start()

    def arrive(name):
        for step, _, receives in steps[name]:
            @pl.when(receives)
            def _():
                step.wait_recv()

    start("f")
    start("r1")
    start("c1")

    for edge, at_edge in (
        ((slice(None), below), me_r == 0),
        ((slice(None), above), me_r == n_row - 1),
    ):
        @pl.when(at_edge)
        def _():
            for slot in range(slots):
                grid[(slot, edge[1], pl.ds(0, own_cps))] = jnp.zeros(
                    (own_cps,) + grid.shape[3:], grid.dtype)
    for place, at_edge in ((left, me_c == 0), (right, me_c == n_col - 1)):
        @pl.when(at_edge)
        def _():
            for slot in range(slots):
                grid[slot, :, place] = jnp.zeros((grid.shape[1],) + grid.shape[3:], grid.dtype)
    if slots - own_frames == 2:
        for place, at_edge in ((low_slot, me_f == 0), (high_slot, me_f == n_frame - 1)):
            @pl.when(at_edge)
            def _():
                for pair in range(own_rps):
                    grid[place, pair, pl.ds(0, own_cps)] = jnp.zeros(
                        (own_cps,) + grid.shape[3:], grid.dtype)

    arrive("r1")
    start("c2")

    keys = bias.shape[2]
    shape = (tokens, keys)
    rows, columns = 2 * own_rps, 2 * own_cps
    at = lax.broadcasted_iota(jnp.int32, shape, 0)
    q_f = jnp.zeros(shape, jnp.int32)
    for f in range(1, own_frames):
        q_f += (at >= f * rows * columns).astype(jnp.int32)
    at = at - q_f * (rows * columns)
    q_r = jnp.zeros(shape, jnp.int32)
    for r in range(1, rows):
        q_r += (at >= r * columns).astype(jnp.int32)
    q_c = at - q_r * columns
    lane = lax.broadcasted_iota(jnp.int32, shape, 1)
    slot = lane >> 7
    pair_r = (lane >> 5) & 3
    pair_c = (lane >> 2) & 7
    if slots - own_frames == 1:
        halo_at = jnp.where(me_f == 0, own_frames, -1)
        k_f = jnp.where(slot == own_frames, halo_at, slot)
    else:
        k_f = jnp.where(slot == low_slot, -1, slot)
        k_f = jnp.where(slot == high_slot, own_frames, k_f)
    pair_r = jnp.where(pair_r == below, -1, jnp.where(pair_r == above, own_rps, pair_r))
    pair_c = jnp.where(pair_c == left, -1, jnp.where(pair_c == right, own_cps, pair_c))
    k_r = 2 * pair_r + ((lane >> 1) & 1)
    k_c = 2 * pair_c + (lane & 1)
    g_f = k_f + me_f * own_frames
    g_r = k_r + me_r * rows
    g_c = k_c + me_c * columns
    inside = (
        (g_f >= 0) & (g_f < n_frame * own_frames)
        & (g_r >= 0) & (g_r < n_row * rows)
        & (g_c >= 0) & (g_c < n_col * columns)
    )
    d_f = jnp.where(inside, jnp.abs(k_f - q_f), 1000)
    d_r = jnp.abs(k_r - q_r)
    d_c = jnp.abs(k_c - q_c)

    def make_bias(head, carry):
        ok = (d_f <= win_ref[head, 0]) & (d_r <= win_ref[head, 1]) & (d_c <= win_ref[head, 2])
        bias[head] = jnp.where(ok, jnp.float32(0), jnp.float32(-1e30))
        return carry

    lax.fori_loop(0, QUARTERS * groups, make_bias, 0)

    arrive("f")
    start("r2")
    arrive("r2")
    start("c3")
    own_copy.wait()
    arrive("c1")
    arrive("c2")
    arrive("c3")

    granules = slots * grid.shape[1] * grid.shape[2]
    scale = 1.0 / math.sqrt(HEAD_DIM)

    def attn_copy(j, k):
        peer = lax.rem(me_c + k, n_col)
        return pltpu.make_async_remote_copy(
            src_ref=attn.at[j, me_c], dst_ref=attn.at[j, me_c],
            send_sem=attn_send.at[j, k], recv_sem=attn_recv.at[j, k],
            device_id={"fsdp": peer}, device_id_type=MESH,
        )

    def attn_arrival(j, k):
        peer = lax.rem(me_c - k + n_col, n_col)
        return pltpu.make_async_remote_copy(
            src_ref=attn.at[j, me_c], dst_ref=attn.at[j, peer],
            send_sem=attn_send.at[j, k], recv_sem=attn_recv.at[j, k],
            device_id={"fsdp": peer}, device_id_type=MESH,
        )

    for j in range(groups):
        lanes = pl.ds(j * 2 * HEAD_DIM, 2 * HEAD_DIM)
        block = grid[:, :, :, :, lanes].astype(jnp.float32)
        block = block.reshape(granules // 2, 2, 2, 8, 2 * HEAD_DIM)
        first, second = block[:, 0], block[:, 1]
        flat = (granules // 2 * 2 * 8, 2 * HEAD_DIM)
        turned_first = pltpu.roll(block[:, 0].reshape(-1, 8, 2 * HEAD_DIM), 4, 1).reshape(first.shape)
        turned_second = pltpu.roll(block[:, 1].reshape(-1, 8, 2 * HEAD_DIM), 4, 1).reshape(first.shape)
        upper = lax.broadcasted_iota(jnp.int32, first.shape, 2) < 4
        even = jnp.where(upper, first, turned_second)
        odd = jnp.where(upper, turned_first, second)
        for quarter in range(QUARTERS):
            head = quarter * groups + j
            dense = (even, odd)[quarter % 2][:, quarter // 2].reshape(keys, 2 * HEAD_DIM)
            dense = dense.astype(jnp.bfloat16)
            query = q_ref[:, pl.ds(head * HEAD_DIM, HEAD_DIM)]
            scores = lax.dot_general(
                query, dense[:, :HEAD_DIM], (((1,), (1,)), ((), ())),
                preferred_element_type=jnp.float32,
            )
            scores = scores * scale + bias[head]
            exponent = jnp.exp(scores - jnp.max(scores, axis=-1, keepdims=True))
            denominator = jnp.sum(exponent, axis=-1, keepdims=True)
            weights = (exponent * (1.0 / denominator)).astype(jnp.bfloat16)
            result = jnp.dot(weights, dense[:, HEAD_DIM:], preferred_element_type=jnp.float32)
            attn[j, me_c, :, pl.ds(quarter * HEAD_DIM, HEAD_DIM)] = result.astype(jnp.bfloat16)

        def send(k, carry):
            attn_copy(j, k).start()
            return carry

        lax.fori_loop(1, n_col, send, 0)

    w_copy.wait()
    total = None
    width = w_ref.shape[1]
    for j in range(groups):
        def gather(k, carry):
            attn_arrival(j, k).wait_recv()
            return carry

        lax.fori_loop(1, n_col, gather, 0)
        weight = jnp.concatenate(
            [w_ref[pl.ds((quarter * groups + j) * HEAD_DIM, HEAD_DIM), :] for quarter in range(QUARTERS)],
            axis=0,
        )
        part = jnp.dot(
            attn[j].reshape(n_col * tokens, QUARTERS * HEAD_DIM), weight,
            preferred_element_type=jnp.float32,
        )
        total = part if total is None else total + part
    y_out[...] = (total * gate_ref[...]).astype(jnp.bfloat16).reshape(n_col, tokens, width)

    def y_copy(k):
        peer = lax.rem(me_c + k, n_col)
        return pltpu.make_async_remote_copy(
            src_ref=y_out.at[peer], dst_ref=y_in.at[me_c],
            send_sem=y_send.at[k], recv_sem=y_recv.at[k],
            device_id={"fsdp": peer}, device_id_type=MESH,
        )

    def y_start(k, carry):
        y_copy(k).start()
        return carry

    def y_wait(k, carry):
        peer = lax.rem(me_c - k + n_col, n_col)
        pltpu.make_async_remote_copy(
            src_ref=y_out.at[peer], dst_ref=y_in.at[peer],
            send_sem=y_send.at[k], recv_sem=y_recv.at[k],
            device_id={"fsdp": peer}, device_id_type=MESH,
        ).wait_recv()
        return carry

    lax.fori_loop(1, n_col, y_start, 0)
    y_in[me_c] = y_out[me_c]
    lax.fori_loop(1, n_col, y_wait, 0)
    out_ref[...] = y_in[...]

    for name in steps:
        for step, sends, _ in steps[name]:
            @pl.when(sends)
            def _():
                step.wait_send()
    for j in range(groups):
        def sent(k, carry):
            attn_copy(j, k).wait_send()
            return carry

        lax.fori_loop(1, n_col, sent, 0)

    def y_sent(k, carry):
        y_copy(k).wait_send()
        return carry

    lax.fori_loop(1, n_col, y_sent, 0)


def body(query, key_value, out_weight, mod_table, step, window):
    frames, rows, columns, features = query.shape
    heads = features // HEAD_DIM
    groups = heads // QUARTERS
    tokens = frames * rows * columns
    width = out_weight.shape[1]
    n_frame, n_row, n_col = (lax.axis_size(a) for a in ("frame", "row", "fsdp"))
    slots = frames + (1 if n_frame == 2 else 2)
    pairs = key_value.reshape(
        2, frames, rows // 2, 2, columns // 2, 2, QUARTERS, groups, HEAD_DIM)
    granules = pairs.transpose(1, 2, 4, 6, 3, 5, 7, 0, 8).reshape(
        frames, rows // 2, columns // 2, QUARTERS * 4, groups * 2 * HEAD_DIM)
    gate = lax.dynamic_slice(mod_table, (step[0], lax.axis_index("fsdp") * width), (1, width))
    block = (slots, rows // 2 + 2, columns // 2 + 2)
    keys = block[0] * block[1] * block[2] * 4
    vmem = pl.BlockSpec(memory_space=pltpu.VMEM)
    out = pl.pallas_call(
        functools.partial(kernel, (n_frame, n_row, n_col)),
        out_shape=jax.ShapeDtypeStruct((n_col, tokens, width), jnp.bfloat16),
        in_specs=[vmem, vmem, pl.BlockSpec(memory_space=pl.ANY), vmem,
                  pl.BlockSpec(memory_space=pltpu.SMEM)],
        out_specs=vmem,
        scratch_shapes=[
            pltpu.VMEM(block + granules.shape[3:], jnp.bfloat16),
            pltpu.VMEM((heads, tokens, keys), jnp.float32),
            pltpu.VMEM((groups, n_col, tokens, QUARTERS * HEAD_DIM), jnp.bfloat16),
            pltpu.VMEM(out_weight.shape, jnp.bfloat16),
            pltpu.VMEM((n_col, tokens, width), jnp.bfloat16),
            pltpu.VMEM((n_col, tokens, width), jnp.bfloat16),
            pltpu.SemaphoreType.DMA((12,)),
            pltpu.SemaphoreType.DMA((12,)),
            pltpu.SemaphoreType.DMA((groups, n_col)),
            pltpu.SemaphoreType.DMA((groups, n_col)),
            pltpu.SemaphoreType.DMA((n_col,)),
            pltpu.SemaphoreType.DMA((n_col,)),
            pltpu.SemaphoreType.DMA((2,)),
        ],
        compiler_params=pltpu.CompilerParams(
            collective_id=0, has_side_effects=True, vmem_limit_bytes=48 * 1024 * 1024),
    )(granules, query.reshape(tokens, features), out_weight, gate, window)
    mixed = out.transpose(1, 0, 2).reshape(tokens, n_col * width)
    return mixed.reshape(frames, rows, columns, -1)


def solution(mesh):
    return jax.shard_map(
        body,
        mesh=mesh,
        in_specs=(
            P("frame", "row", "fsdp", None),
            P(None, "frame", "row", "fsdp", None),
            P(None, "fsdp"),
            P(),
            P(),
            P(),
        ),
        out_specs=P("frame", "row", "fsdp", None),
        check_vma=False,
    )
```

```python
import functools
import math

import jax
import jax.numpy as jnp
from jax import lax
from jax.experimental import pallas as pl
from jax.experimental.pallas import tpu as pltpu
from jax.sharding import PartitionSpec as P

HEAD_DIM = 128
QUARTERS = 4
CHUNKS = ((0, 5),)
MESH = pl.DeviceIdType.MESH


def kernel(
    sizes, gin, q_ref, w_hbm, gate_ref, win_ref, out_ref,
    grid, bias, attn, w_ref, total, y_out, y_in,
    halo_send, halo_recv, attn_send, attn_recv, y_send, y_recv, local_sem,
):
    n_frame, n_row, n_col = sizes
    slots = grid.shape[0]
    groups = gin.shape[4] // (2 * HEAD_DIM)
    tokens = q_ref.shape[0]
    count = tokens // gin.shape[0]
    own_frames, own_rps, own_cps = gin.shape[:3]
    me_f = lax.axis_index("frame")
    me_r = lax.axis_index("row")
    me_c = lax.axis_index("fsdp")

    w_copy = pltpu.make_async_copy(w_hbm, w_ref, local_sem.at[0])
    w_copy.start()
    own_copy = pltpu.make_async_copy(
        gin, grid.at[pl.ds(0, own_frames), pl.ds(0, own_rps), pl.ds(0, own_cps)], local_sem.at[1]
    )
    own_copy.start()

    barrier = pltpu.get_barrier_semaphore()

    def neighbours(axis, me, count):
        return ((axis, me + 1, me < count - 1), (axis, me - 1, me > 0))

    near = neighbours("frame", me_f, n_frame) + neighbours("row", me_r, n_row)
    for axis, other, there in near:
        @pl.when(there)
        def _():
            pl.semaphore_signal(barrier, inc=1, device_id={axis: other}, device_id_type=MESH)

    def greet(k, carry):
        peer = lax.rem(me_c + k, n_col)
        pl.semaphore_signal(barrier, inc=1, device_id={"fsdp": peer}, device_id_type=MESH)
        return carry

    lax.fori_loop(1, n_col, greet, 0)
    greetings = n_col - 1
    for _, _, there in near:
        greetings += there.astype(jnp.int32)
    pl.semaphore_wait(barrier, greetings)

    def copy(src, dst, index, axis, other):
        return pltpu.make_async_remote_copy(
            src_ref=src, dst_ref=dst, send_sem=halo_send.at[index], recv_sem=halo_recv.at[index],
            device_id={axis: other}, device_id_type=MESH,
        )

    own_f = pl.ds(0, own_frames)
    halo_f = pl.ds(own_frames, slots - own_frames)
    own_r = pl.ds(0, own_rps)
    halo_r = pl.ds(own_rps, 2)
    own_c = pl.ds(0, own_cps)
    below, above = own_rps, own_rps + 1
    left, right = own_cps, own_cps + 1
    low_slot, high_slot = own_frames, slots - 1
    steps = {}

    def add(name, axis, me, count, index, up, down):
        steps[name] = (
            (copy(up[0], up[1], index, axis, me + 1), me < count - 1, me > 0),
            (copy(down[0], down[1], index + 1, axis, me - 1), me > 0, me < count - 1),
        )

    every = slice(None)
    all_r = pl.ds(0, own_rps + 2)
    for part, (low, high) in enumerate(CHUNKS):
        base = 12 * part
        tail = (every, pl.ds(low * 2 * HEAD_DIM, (high - low) * 2 * HEAD_DIM))

        def own(*place):
            return gin.at[place + tail]

        def held(*place):
            return grid.at[place + tail]

        add(("f", part), "frame", me_f, n_frame, base,
            (own(own_frames - 1, every, every), held(low_slot, own_r, own_c)),
            (own(0, every, every), held(high_slot, own_r, own_c)))
        add(("r1", part), "row", me_r, n_row, base + 2,
            (own(every, own_rps - 1, every), held(own_f, below, own_c)),
            (own(every, 0, every), held(own_f, above, own_c)))
        add(("r2", part), "row", me_r, n_row, base + 4,
            (held(halo_f, own_rps - 1, own_c), held(halo_f, below, own_c)),
            (held(halo_f, 0, own_c), held(halo_f, above, own_c)))
        add(("c1", part), "fsdp", me_c, n_col, base + 6,
            (own(every, every, own_cps - 1), held(own_f, own_r, left)),
            (own(every, every, 0), held(own_f, own_r, right)))
        add(("c2", part), "fsdp", me_c, n_col, base + 8,
            (held(own_f, halo_r, own_cps - 1), held(own_f, halo_r, left)),
            (held(own_f, halo_r, 0), held(own_f, halo_r, right)))
        add(("c3", part), "fsdp", me_c, n_col, base + 10,
            (held(halo_f, all_r, own_cps - 1), held(halo_f, all_r, left)),
            (held(halo_f, all_r, 0), held(halo_f, all_r, right)))

    def start(name, part):
        for step, sends, _ in steps[name, part]:
            @pl.when(sends)
            def _():
                step.start()

    def arrive(name, part):
        for step, _, receives in steps[name, part]:
            @pl.when(receives)
            def _():
                step.wait_recv()

    start("f", 0)
    start("r1", 0)
    start("c1", 0)

    for edge, at_edge in (
        ((slice(None), below), me_r == 0),
        ((slice(None), above), me_r == n_row - 1),
    ):
        @pl.when(at_edge)
        def _():
            for slot in range(slots):
                grid[(slot, edge[1], pl.ds(0, own_cps))] = jnp.zeros(
                    (own_cps,) + grid.shape[3:], grid.dtype)
    for place, at_edge in ((left, me_c == 0), (right, me_c == n_col - 1)):
        @pl.when(at_edge)
        def _():
            for slot in range(slots):
                grid[slot, :, place] = jnp.zeros((grid.shape[1],) + grid.shape[3:], grid.dtype)
    if slots - own_frames == 2:
        for place, at_edge in ((low_slot, me_f == 0), (high_slot, me_f == n_frame - 1)):
            @pl.when(at_edge)
            def _():
                for pair in range(own_rps):
                    grid[place, pair, pl.ds(0, own_cps)] = jnp.zeros(
                        (own_cps,) + grid.shape[3:], grid.dtype)

    arrive("r1", 0)
    start("c2", 0)

    keys = bias.shape[2]
    shape = (tokens, keys)
    rows, columns = 2 * own_rps, 2 * own_cps
    at = lax.broadcasted_iota(jnp.int32, shape, 0)
    q_f = jnp.zeros(shape, jnp.int32)
    for f in range(1, own_frames):
        q_f += (at >= f * rows * columns).astype(jnp.int32)
    at = at - q_f * (rows * columns)
    q_r = jnp.zeros(shape, jnp.int32)
    for r in range(1, rows):
        q_r += (at >= r * columns).astype(jnp.int32)
    q_c = at - q_r * columns
    lane = lax.broadcasted_iota(jnp.int32, shape, 1)
    slot = lane >> 7
    pair_r = (lane >> 5) & 3
    pair_c = (lane >> 2) & 7
    if slots - own_frames == 1:
        halo_at = jnp.where(me_f == 0, own_frames, -1)
        k_f = jnp.where(slot == own_frames, halo_at, slot)
    else:
        k_f = jnp.where(slot == low_slot, -1, slot)
        k_f = jnp.where(slot == high_slot, own_frames, k_f)
    pair_r = jnp.where(pair_r == below, -1, jnp.where(pair_r == above, own_rps, pair_r))
    pair_c = jnp.where(pair_c == left, -1, jnp.where(pair_c == right, own_cps, pair_c))
    k_r = 2 * pair_r + ((lane >> 1) & 1)
    k_c = 2 * pair_c + (lane & 1)
    g_f = k_f + me_f * own_frames
    g_r = k_r + me_r * rows
    g_c = k_c + me_c * columns
    inside = (
        (g_f >= 0) & (g_f < n_frame * own_frames)
        & (g_r >= 0) & (g_r < n_row * rows)
        & (g_c >= 0) & (g_c < n_col * columns)
    )
    d_f = jnp.where(inside, jnp.abs(k_f - q_f), 1000)
    d_r = jnp.abs(k_r - q_r)
    d_c = jnp.abs(k_c - q_c)

    def make_bias(head, carry):
        ok = (d_f <= win_ref[head, 0]) & (d_r <= win_ref[head, 1]) & (d_c <= win_ref[head, 2])
        bias[head] = jnp.where(ok, jnp.float32(0), jnp.float32(-1e30))
        return carry

    lax.fori_loop(0, QUARTERS * groups, make_bias, 0)

    own_copy.wait()
    arrive("c1", 0)
    arrive("c2", 0)

    apart = n_frame == 2

    def frame_at(turn):
        if not apart:
            return turn
        return me_f if turn == 0 else own_frames - 1 - me_f

    def frame_rows(turn):
        return pl.ds(pl.multiple_of(frame_at(turn) * count, 16), count)

    def relay(number):
        if number == 0:
            arrive("f", 0)
            start("r2", 0)
        else:
            arrive("r2", 0)
            start("c3", 0)

    if not apart:
        relay(0)
        relay(1)
        arrive("c3", 0)

    pairs = grid.shape[1] * grid.shape[2]
    scale = 1.0 / math.sqrt(HEAD_DIM)

    def block_copy(j, origin, way):
        other = me_c + 1 - 2 * way
        return pltpu.make_async_remote_copy(
            src_ref=attn.at[j, origin], dst_ref=attn.at[j, origin],
            send_sem=attn_send.at[j, way, origin], recv_sem=attn_recv.at[j, origin],
            device_id={"fsdp": other}, device_id_type=MESH,
        )

    def wait_block(j, origin):
        block_copy(j, origin, 0).wait_recv()

    passes = (me_c < n_col - 1, me_c > 0)

    def attend(turn):
        used = own_frames if apart and turn == 0 else slots
        for j in range(groups):
            if apart and turn == 0 and j in (1, 3):
                relay(j // 2)
            attend_group(turn, j, used)

    def attend_group(turn, j, used):
        granules = used * pairs
        length = granules * 4
        rows = frame_rows(turn)
        lanes = pl.ds(j * 2 * HEAD_DIM, 2 * HEAD_DIM)
        block = grid[pl.ds(0, used), :, :, :, lanes].astype(jnp.float32)
        block = block.reshape(granules // 2, 2, 2, 8, 2 * HEAD_DIM)
        first, second = block[:, 0], block[:, 1]
        turned_first = pltpu.roll(block[:, 0].reshape(-1, 8, 2 * HEAD_DIM), 4, 1).reshape(first.shape)
        turned_second = pltpu.roll(block[:, 1].reshape(-1, 8, 2 * HEAD_DIM), 4, 1).reshape(first.shape)
        upper = lax.broadcasted_iota(jnp.int32, first.shape, 2) < 4
        even = jnp.where(upper, first, turned_second)
        odd = jnp.where(upper, turned_first, second)
        for quarter in range(QUARTERS):
            head = quarter * groups + j
            dense = (even, odd)[quarter % 2][:, quarter // 2].reshape(length, 2 * HEAD_DIM)
            dense = dense.astype(jnp.bfloat16)
            query = q_ref[rows, pl.ds(head * HEAD_DIM, HEAD_DIM)]
            scores = lax.dot_general(
                query, dense[:, :HEAD_DIM], (((1,), (1,)), ((), ())),
                preferred_element_type=jnp.float32,
            )
            scores = scores * scale + bias[head, rows, pl.ds(0, length)]
            exponent = jnp.exp(scores - jnp.max(scores, axis=-1, keepdims=True))
            denominator = jnp.sum(exponent, axis=-1, keepdims=True)
            weights = (exponent * (1.0 / denominator)).astype(jnp.bfloat16)
            result = jnp.dot(weights, dense[:, HEAD_DIM:], preferred_element_type=jnp.float32)
            attn[turn * groups + j, me_c, :, pl.ds(quarter * HEAD_DIM, HEAD_DIM)] = result.astype(jnp.bfloat16)

        for way in range(2):
            @pl.when(passes[way])
            def _():
                block_copy(turn * groups + j, me_c, way).start()

    def y_copy(turn, peer):
        return pltpu.make_async_remote_copy(
            src_ref=y_out.at[turn, peer], dst_ref=y_in.at[turn, me_c],
            send_sem=y_send.at[turn, peer], recv_sem=y_recv.at[turn, me_c],
            device_id={"fsdp": peer}, device_id_type=MESH,
        )

    def product(turn, j, origin):
        weight = jnp.concatenate(
            [w_ref[pl.ds((quarter * groups + j) * HEAD_DIM, HEAD_DIM), :]
             for quarter in range(QUARTERS)], axis=0)
        return jnp.dot(attn[turn * groups + j, origin], weight, preferred_element_type=jnp.float32)

    def distance(turn, d, carry):
        origins = (me_c - d, me_c + d)
        there = (origins[0] >= 0, origins[1] < n_col)
        for j in range(groups):
            for way in range(2):
                @pl.when(there[way])
                def _():
                    wait_block(turn * groups + j, origins[way])

                    @pl.when(passes[way])
                    def _():
                        block_copy(turn * groups + j, origins[way], way).start()
            for way in range(2):
                @pl.when(there[way])
                def _():
                    part = product(turn, j, origins[way])
                    if j > 0:
                        part = total[way] + part
                    if j < groups - 1:
                        total[way] = part
                    else:
                        y_out[turn, origins[way]] = (part * gate_ref[...]).astype(jnp.bfloat16)
                        y_copy(turn, origins[way]).start()
        return carry

    turns = own_frames
    attend(0)
    w_copy.wait()
    distance(0, 1, 0)
    if apart:
        arrive("c3", 0)
    for turn in range(1, turns):
        attend(turn)
    for turn in range(turns):
        lax.fori_loop(2 if turn == 0 else 1, n_col, functools.partial(distance, turn), 0)
    for turn in range(turns):
        mine = product(turn, 0, me_c)
        for j in range(1, groups):
            mine += product(turn, j, me_c)
        y_in[turn, me_c] = (mine * gate_ref[...]).astype(jnp.bfloat16)

    for turn in range(turns):
        def y_wait(k, carry):
            peer = lax.rem(me_c + k, n_col)
            pltpu.make_async_remote_copy(
                src_ref=y_out.at[turn, peer], dst_ref=y_in.at[turn, peer],
                send_sem=y_send.at[turn, peer], recv_sem=y_recv.at[turn, peer],
                device_id={"fsdp": peer}, device_id_type=MESH,
            ).wait_recv()
            return carry

        lax.fori_loop(1, n_col, y_wait, 0)
        out_ref[:, frame_rows(turn), :] = y_in[turn]

    for name in steps:
        for step, sends, _ in steps[name]:
            @pl.when(sends)
            def _():
                step.wait_send()
    for number in range(turns * groups):
        for way in range(2):
            def sent(d, carry):
                origin = me_c - d + 2 * d * way

                @pl.when(passes[way] & (origin >= 0) & (origin < n_col))
                def _():
                    block_copy(number, origin, way).wait_send()
                return carry

            lax.fori_loop(0, n_col, sent, 0)
    for turn in range(turns):
        def y_sent(k, carry):
            y_copy(turn, lax.rem(me_c + k, n_col)).wait_send()
            return carry

        lax.fori_loop(1, n_col, y_sent, 0)


def body(query, key_value, out_weight, mod_table, step, window):
    frames, rows, columns, features = query.shape
    heads = features // HEAD_DIM
    groups = heads // QUARTERS
    tokens = frames * rows * columns
    width = out_weight.shape[1]
    n_frame, n_row, n_col = (lax.axis_size(a) for a in ("frame", "row", "fsdp"))
    slots = frames + (1 if n_frame == 2 else 2)
    pairs = key_value.reshape(
        2, frames, rows // 2, 2, columns // 2, 2, QUARTERS, groups, HEAD_DIM)
    granules = pairs.transpose(1, 2, 4, 6, 3, 5, 7, 0, 8).reshape(
        frames, rows // 2, columns // 2, QUARTERS * 4, groups * 2 * HEAD_DIM)
    gate = lax.dynamic_slice(mod_table, (step[0], lax.axis_index("fsdp") * width), (1, width))
    block = (slots, rows // 2 + 2, columns // 2 + 2)
    keys = block[0] * block[1] * block[2] * 4
    vmem = pl.BlockSpec(memory_space=pltpu.VMEM)
    out = pl.pallas_call(
        functools.partial(kernel, (n_frame, n_row, n_col)),
        out_shape=jax.ShapeDtypeStruct((n_col, tokens, width), jnp.bfloat16),
        in_specs=[vmem, vmem, pl.BlockSpec(memory_space=pl.ANY), vmem,
                  pl.BlockSpec(memory_space=pltpu.SMEM)],
        out_specs=vmem,
        scratch_shapes=[
            pltpu.VMEM(block + granules.shape[3:], jnp.bfloat16),
            pltpu.VMEM((heads, tokens, keys), jnp.float32),
            pltpu.VMEM((frames * groups, n_col, tokens // frames, QUARTERS * HEAD_DIM), jnp.bfloat16),
            pltpu.VMEM(out_weight.shape, jnp.bfloat16),
            pltpu.VMEM((2, tokens // frames, width), jnp.float32),
            pltpu.VMEM((frames, n_col, tokens // frames, width), jnp.bfloat16),
            pltpu.VMEM((frames, n_col, tokens // frames, width), jnp.bfloat16),
            pltpu.SemaphoreType.DMA((12 * len(CHUNKS),)),
            pltpu.SemaphoreType.DMA((12 * len(CHUNKS),)),
            pltpu.SemaphoreType.DMA((frames * groups, 2, n_col)),
            pltpu.SemaphoreType.DMA((frames * groups, n_col)),
            pltpu.SemaphoreType.DMA((frames, n_col)),
            pltpu.SemaphoreType.DMA((frames, n_col)),
            pltpu.SemaphoreType.DMA((2,)),
        ],
        compiler_params=pltpu.CompilerParams(
            collective_id=0, has_side_effects=True, vmem_limit_bytes=61 * 1024 * 1024),
    )(granules, query.reshape(tokens, features), out_weight, gate, window)
    mixed = out.transpose(1, 0, 2).reshape(tokens, n_col * width)
    return mixed.reshape(frames, rows, columns, -1)


def solution(mesh):
    return jax.shard_map(
        body,
        mesh=mesh,
        in_specs=(
            P("frame", "row", "fsdp", None),
            P(None, "frame", "row", "fsdp", None),
            P(None, "fsdp"),
            P(),
            P(),
            P(),
        ),
        out_specs=P("frame", "row", "fsdp", None),
        check_vma=False,
    )
```

```python
import functools
import math

import jax
import jax.numpy as jnp
from jax import lax
from jax.experimental import pallas as pl
from jax.experimental.pallas import tpu as pltpu
from jax.sharding import PartitionSpec as P

HEAD_DIM = 128
QUARTERS = 4
CHUNKS = ((0, 5),)
MESH = pl.DeviceIdType.MESH


def kernel(
    sizes, gin, q_ref, w_hbm, mod_ref, step_ref, win_ref, out_ref,
    grid, bias, attn, w_ref, total, y_out, y_in,
    halo_send, halo_recv, attn_send, attn_recv, y_send, y_recv, local_sem,
):
    n_frame, n_row, n_col = sizes
    slots = grid.shape[0]
    groups = gin.shape[4] // (2 * HEAD_DIM)
    tokens = q_ref.shape[0]
    count = tokens // gin.shape[0]
    own_frames, own_rps, own_cps = gin.shape[:3]
    me_f = lax.axis_index("frame")
    me_r = lax.axis_index("row")
    me_c = lax.axis_index("fsdp")

    w_copy = pltpu.make_async_copy(w_hbm, w_ref, local_sem.at[0])
    w_copy.start()
    own_copy = pltpu.make_async_copy(
        gin, grid.at[pl.ds(0, own_frames), pl.ds(0, own_rps), pl.ds(0, own_cps)], local_sem.at[1]
    )
    own_copy.start()

    barrier = pltpu.get_barrier_semaphore()

    def neighbours(axis, me, count):
        return ((axis, me + 1, me < count - 1), (axis, me - 1, me > 0))

    near = neighbours("frame", me_f, n_frame) + neighbours("row", me_r, n_row)
    for axis, other, there in near:
        @pl.when(there)
        def _():
            pl.semaphore_signal(barrier, inc=1, device_id={axis: other}, device_id_type=MESH)

    def greet(k, carry):
        peer = lax.rem(me_c + k, n_col)
        pl.semaphore_signal(barrier, inc=1, device_id={"fsdp": peer}, device_id_type=MESH)
        return carry

    lax.fori_loop(1, n_col, greet, 0)
    greetings = n_col - 1
    for _, _, there in near:
        greetings += there.astype(jnp.int32)
    pl.semaphore_wait(barrier, greetings)

    def copy(src, dst, index, axis, other):
        return pltpu.make_async_remote_copy(
            src_ref=src, dst_ref=dst, send_sem=halo_send.at[index], recv_sem=halo_recv.at[index],
            device_id={axis: other}, device_id_type=MESH,
        )

    own_f = pl.ds(0, own_frames)
    halo_f = pl.ds(own_frames, slots - own_frames)
    own_r = pl.ds(0, own_rps)
    halo_r = pl.ds(own_rps, 2)
    own_c = pl.ds(0, own_cps)
    below, above = own_rps, own_rps + 1
    left, right = own_cps, own_cps + 1
    low_slot, high_slot = own_frames, slots - 1
    steps = {}

    def add(name, axis, me, count, index, up, down):
        steps[name] = (
            (copy(up[0], up[1], index, axis, me + 1), me < count - 1, me > 0),
            (copy(down[0], down[1], index + 1, axis, me - 1), me > 0, me < count - 1),
        )

    every = slice(None)
    all_r = pl.ds(0, own_rps + 2)
    for part, (low, high) in enumerate(CHUNKS):
        base = 12 * part
        tail = (every, pl.ds(low * 2 * HEAD_DIM, (high - low) * 2 * HEAD_DIM))

        def own(*place):
            return gin.at[place + tail]

        def held(*place):
            return grid.at[place + tail]

        add(("f", part), "frame", me_f, n_frame, base,
            (own(own_frames - 1, every, every), held(low_slot, own_r, own_c)),
            (own(0, every, every), held(high_slot, own_r, own_c)))
        add(("r1", part), "row", me_r, n_row, base + 2,
            (own(every, own_rps - 1, every), held(own_f, below, own_c)),
            (own(every, 0, every), held(own_f, above, own_c)))
        add(("r2", part), "row", me_r, n_row, base + 4,
            (held(halo_f, own_rps - 1, own_c), held(halo_f, below, own_c)),
            (held(halo_f, 0, own_c), held(halo_f, above, own_c)))
        add(("c1", part), "fsdp", me_c, n_col, base + 6,
            (own(every, every, own_cps - 1), held(own_f, own_r, left)),
            (own(every, every, 0), held(own_f, own_r, right)))
        add(("c2", part), "fsdp", me_c, n_col, base + 8,
            (held(own_f, halo_r, own_cps - 1), held(own_f, halo_r, left)),
            (held(own_f, halo_r, 0), held(own_f, halo_r, right)))
        add(("c3", part), "fsdp", me_c, n_col, base + 10,
            (held(halo_f, all_r, own_cps - 1), held(halo_f, all_r, left)),
            (held(halo_f, all_r, 0), held(halo_f, all_r, right)))

    def start(name, part):
        for step, sends, _ in steps[name, part]:
            @pl.when(sends)
            def _():
                step.start()

    def arrive(name, part):
        for step, _, receives in steps[name, part]:
            @pl.when(receives)
            def _():
                step.wait_recv()

    start("f", 0)
    start("r1", 0)
    start("c1", 0)

    for edge, at_edge in (
        ((slice(None), below), me_r == 0),
        ((slice(None), above), me_r == n_row - 1),
    ):
        @pl.when(at_edge)
        def _():
            for slot in range(slots):
                grid[(slot, edge[1], pl.ds(0, own_cps))] = jnp.zeros(
                    (own_cps,) + grid.shape[3:], grid.dtype)
    for place, at_edge in ((left, me_c == 0), (right, me_c == n_col - 1)):
        @pl.when(at_edge)
        def _():
            for slot in range(slots):
                grid[slot, :, place] = jnp.zeros((grid.shape[1],) + grid.shape[3:], grid.dtype)
    if slots - own_frames == 2:
        for place, at_edge in ((low_slot, me_f == 0), (high_slot, me_f == n_frame - 1)):
            @pl.when(at_edge)
            def _():
                for pair in range(own_rps):
                    grid[place, pair, pl.ds(0, own_cps)] = jnp.zeros(
                        (own_cps,) + grid.shape[3:], grid.dtype)

    arrive("r1", 0)
    start("c2", 0)

    keys = bias.shape[2]
    shape = (tokens, keys)
    rows, columns = 2 * own_rps, 2 * own_cps
    at = lax.broadcasted_iota(jnp.int32, shape, 0)
    q_f = jnp.zeros(shape, jnp.int32)
    for f in range(1, own_frames):
        q_f += (at >= f * rows * columns).astype(jnp.int32)
    at = at - q_f * (rows * columns)
    q_r = jnp.zeros(shape, jnp.int32)
    for r in range(1, rows):
        q_r += (at >= r * columns).astype(jnp.int32)
    q_c = at - q_r * columns
    lane = lax.broadcasted_iota(jnp.int32, shape, 1)
    slot = lane >> 7
    pair_r = (lane >> 5) & 3
    pair_c = (lane >> 2) & 7
    if slots - own_frames == 1:
        halo_at = jnp.where(me_f == 0, own_frames, -1)
        k_f = jnp.where(slot == own_frames, halo_at, slot)
    else:
        k_f = jnp.where(slot == low_slot, -1, slot)
        k_f = jnp.where(slot == high_slot, own_frames, k_f)
    pair_r = jnp.where(pair_r == below, -1, jnp.where(pair_r == above, own_rps, pair_r))
    pair_c = jnp.where(pair_c == left, -1, jnp.where(pair_c == right, own_cps, pair_c))
    k_r = 2 * pair_r + ((lane >> 1) & 1)
    k_c = 2 * pair_c + (lane & 1)
    g_f = k_f + me_f * own_frames
    g_r = k_r + me_r * rows
    g_c = k_c + me_c * columns
    inside = (
        (g_f >= 0) & (g_f < n_frame * own_frames)
        & (g_r >= 0) & (g_r < n_row * rows)
        & (g_c >= 0) & (g_c < n_col * columns)
    )
    d_f = jnp.where(inside, jnp.abs(k_f - q_f), 1000)
    d_r = jnp.abs(k_r - q_r)
    d_c = jnp.abs(k_c - q_c)

    def make_bias(head, carry):
        ok = (d_f <= win_ref[0, head]) & (d_r <= win_ref[1, head]) & (d_c <= win_ref[2, head])
        bias[head] = jnp.where(ok, jnp.float32(0), jnp.float32(-1e30))
        return carry

    lax.fori_loop(0, QUARTERS * groups, make_bias, 0)

    own_copy.wait()
    arrive("c1", 0)
    arrive("c2", 0)

    apart = n_frame == 2

    def frame_at(turn):
        if not apart:
            return turn
        return me_f if turn == 0 else own_frames - 1 - me_f

    def frame_rows(turn):
        return pl.ds(pl.multiple_of(frame_at(turn) * count, 16), count)

    def relay(number):
        if number == 0:
            arrive("f", 0)
            start("r2", 0)
        else:
            arrive("r2", 0)
            start("c3", 0)

    if not apart:
        relay(0)
        relay(1)
        arrive("c3", 0)

    pairs = grid.shape[1] * grid.shape[2]
    scale = 1.0 / math.sqrt(HEAD_DIM)

    def block_copy(j, origin, way):
        other = me_c + 1 - 2 * way
        return pltpu.make_async_remote_copy(
            src_ref=attn.at[j, origin], dst_ref=attn.at[j, origin],
            send_sem=attn_send.at[j, way, origin], recv_sem=attn_recv.at[j, origin],
            device_id={"fsdp": other}, device_id_type=MESH,
        )

    def wait_block(j, origin):
        block_copy(j, origin, 0).wait_recv()

    passes = (me_c < n_col - 1, me_c > 0)

    def attend(turn):
        used = own_frames if apart and turn == 0 else slots
        for j in range(groups):
            if apart and turn == 0 and j in (1, 3):
                relay(j // 2)
            attend_group(turn, j, used)

    def attend_group(turn, j, used):
        granules = used * pairs
        length = granules * 4
        rows = frame_rows(turn)
        lanes = pl.ds(j * 2 * HEAD_DIM, 2 * HEAD_DIM)
        block = grid[pl.ds(0, used), :, :, :, lanes].astype(jnp.float32)
        block = block.reshape(granules // 2, 2, 2, 8, 2 * HEAD_DIM)
        first, second = block[:, 0], block[:, 1]
        turned_first = pltpu.roll(block[:, 0].reshape(-1, 8, 2 * HEAD_DIM), 4, 1).reshape(first.shape)
        turned_second = pltpu.roll(block[:, 1].reshape(-1, 8, 2 * HEAD_DIM), 4, 1).reshape(first.shape)
        upper = lax.broadcasted_iota(jnp.int32, first.shape, 2) < 4
        even = jnp.where(upper, first, turned_second)
        odd = jnp.where(upper, turned_first, second)
        for quarter in range(QUARTERS):
            head = quarter * groups + j
            dense = (even, odd)[quarter % 2][:, quarter // 2].reshape(length, 2 * HEAD_DIM)
            dense = dense.astype(jnp.bfloat16)
            query = q_ref[rows, pl.ds(head * HEAD_DIM, HEAD_DIM)]
            scores = lax.dot_general(
                query, dense[:, :HEAD_DIM], (((1,), (1,)), ((), ())),
                preferred_element_type=jnp.float32,
            )
            scores = scores * scale + bias[head, rows, pl.ds(0, length)]
            exponent = jnp.exp(scores - jnp.max(scores, axis=-1, keepdims=True))
            denominator = jnp.sum(exponent, axis=-1, keepdims=True)
            weights = (exponent * (1.0 / denominator)).astype(jnp.bfloat16)
            result = jnp.dot(weights, dense[:, HEAD_DIM:], preferred_element_type=jnp.float32)
            attn[turn * groups + j, me_c, :, pl.ds(quarter * HEAD_DIM, HEAD_DIM)] = result.astype(jnp.bfloat16)

        for way in range(2):
            @pl.when(passes[way])
            def _():
                block_copy(turn * groups + j, me_c, way).start()

    def y_copy(turn, peer):
        return pltpu.make_async_remote_copy(
            src_ref=y_out.at[turn, peer], dst_ref=y_in.at[turn, me_c],
            send_sem=y_send.at[turn, peer], recv_sem=y_recv.at[turn, me_c],
            device_id={"fsdp": peer}, device_id_type=MESH,
        )

    def product(turn, j, origin):
        weight = jnp.concatenate(
            [w_ref[pl.ds((quarter * groups + j) * HEAD_DIM, HEAD_DIM), :]
             for quarter in range(QUARTERS)], axis=0)
        return jnp.dot(attn[turn * groups + j, origin], weight, preferred_element_type=jnp.float32)

    def distance(turn, d, carry):
        origins = (me_c - d, me_c + d)
        there = (origins[0] >= 0, origins[1] < n_col)
        for j in range(groups):
            for way in range(2):
                @pl.when(there[way])
                def _():
                    wait_block(turn * groups + j, origins[way])

                    @pl.when(passes[way])
                    def _():
                        block_copy(turn * groups + j, origins[way], way).start()
            for way in range(2):
                @pl.when(there[way])
                def _():
                    part = product(turn, j, origins[way])
                    if j > 0:
                        part = total[way] + part
                    if j < groups - 1:
                        total[way] = part
                    else:
                        y_out[turn, origins[way]] = (part * gate).astype(jnp.bfloat16)
                        y_copy(turn, origins[way]).start()
        return carry

    width = w_ref.shape[1]
    table_row = mod_ref[pl.ds(step_ref[0], 1), :]
    gate = table_row[:, :width]
    for place in range(1, n_col):
        gate = jnp.where(me_c == place, table_row[:, place * width:(place + 1) * width], gate)
    turns = own_frames
    attend(0)
    w_copy.wait()
    distance(0, 1, 0)
    if apart:
        arrive("c3", 0)
    for turn in range(1, turns):
        attend(turn)
    for turn in range(turns):
        lax.fori_loop(2 if turn == 0 else 1, n_col, functools.partial(distance, turn), 0)
    for turn in range(turns):
        mine = product(turn, 0, me_c)
        for j in range(1, groups):
            mine += product(turn, j, me_c)
        y_in[turn, me_c] = (mine * gate).astype(jnp.bfloat16)

    for turn in range(turns):
        def y_wait(k, carry):
            peer = lax.rem(me_c + k, n_col)
            pltpu.make_async_remote_copy(
                src_ref=y_out.at[turn, peer], dst_ref=y_in.at[turn, peer],
                send_sem=y_send.at[turn, peer], recv_sem=y_recv.at[turn, peer],
                device_id={"fsdp": peer}, device_id_type=MESH,
            ).wait_recv()
            return carry

        lax.fori_loop(1, n_col, y_wait, 0)
        out_ref[:, frame_rows(turn), :] = y_in[turn]

    for name in steps:
        for step, sends, _ in steps[name]:
            @pl.when(sends)
            def _():
                step.wait_send()
    for number in range(turns * groups):
        for way in range(2):
            def sent(d, carry):
                origin = me_c - d + 2 * d * way

                @pl.when(passes[way] & (origin >= 0) & (origin < n_col))
                def _():
                    block_copy(number, origin, way).wait_send()
                return carry

            lax.fori_loop(0, n_col, sent, 0)
    for turn in range(turns):
        def y_sent(k, carry):
            y_copy(turn, lax.rem(me_c + k, n_col)).wait_send()
            return carry

        lax.fori_loop(1, n_col, y_sent, 0)


def body(query, key_value, out_weight, mod_table, step, window):
    frames, rows, columns, features = query.shape
    heads = features // HEAD_DIM
    groups = heads // QUARTERS
    tokens = frames * rows * columns
    width = out_weight.shape[1]
    n_frame, n_row, n_col = (lax.axis_size(a) for a in ("frame", "row", "fsdp"))
    slots = frames + (1 if n_frame == 2 else 2)
    pairs = key_value.reshape(
        2, frames, rows // 2, 2, columns // 2, 2, QUARTERS, groups, HEAD_DIM)
    granules = pairs.transpose(1, 2, 4, 6, 3, 5, 7, 0, 8).reshape(
        frames, rows // 2, columns // 2, QUARTERS * 4, groups * 2 * HEAD_DIM)
    block = (slots, rows // 2 + 2, columns // 2 + 2)
    keys = block[0] * block[1] * block[2] * 4
    vmem = pl.BlockSpec(memory_space=pltpu.VMEM)
    out = pl.pallas_call(
        functools.partial(kernel, (n_frame, n_row, n_col)),
        out_shape=jax.ShapeDtypeStruct((n_col, tokens, width), jnp.bfloat16),
        in_specs=[vmem, vmem, pl.BlockSpec(memory_space=pl.ANY), vmem,
                  pl.BlockSpec(memory_space=pltpu.SMEM), pl.BlockSpec(memory_space=pltpu.SMEM)],
        out_specs=vmem,
        scratch_shapes=[
            pltpu.VMEM(block + granules.shape[3:], jnp.bfloat16),
            pltpu.VMEM((heads, tokens, keys), jnp.float32),
            pltpu.VMEM((frames * groups, n_col, tokens // frames, QUARTERS * HEAD_DIM), jnp.bfloat16),
            pltpu.VMEM(out_weight.shape, jnp.bfloat16),
            pltpu.VMEM((2, tokens // frames, width), jnp.float32),
            pltpu.VMEM((frames, n_col, tokens // frames, width), jnp.bfloat16),
            pltpu.VMEM((frames, n_col, tokens // frames, width), jnp.bfloat16),
            pltpu.SemaphoreType.DMA((12 * len(CHUNKS),)),
            pltpu.SemaphoreType.DMA((12 * len(CHUNKS),)),
            pltpu.SemaphoreType.DMA((frames * groups, 2, n_col)),
            pltpu.SemaphoreType.DMA((frames * groups, n_col)),
            pltpu.SemaphoreType.DMA((frames, n_col)),
            pltpu.SemaphoreType.DMA((frames, n_col)),
            pltpu.SemaphoreType.DMA((2,)),
        ],
        compiler_params=pltpu.CompilerParams(
            collective_id=0, has_side_effects=True, vmem_limit_bytes=40 * 1024 * 1024),
    )(granules, query.reshape(tokens, features), out_weight, mod_table, step, window.T)
    mixed = out.transpose(1, 0, 2).reshape(tokens, n_col * width)
    return mixed.reshape(frames, rows, columns, -1)


def solution(mesh):
    return jax.shard_map(
        body,
        mesh=mesh,
        in_specs=(
            P("frame", "row", "fsdp", None),
            P(None, "frame", "row", "fsdp", None),
            P(None, "fsdp"),
            P(),
            P(),
            P(),
        ),
        out_specs=P("frame", "row", "fsdp", None),
        check_vma=False,
    )
```

```python
import functools
import math

import jax
import jax.numpy as jnp
from jax import lax
from jax.experimental import pallas as pl
from jax.experimental.pallas import tpu as pltpu
from jax.sharding import PartitionSpec as P

HEAD_DIM = 128
QUARTERS = 4
CHUNKS = ((0, 5),)
MESH = pl.DeviceIdType.MESH


def kernel(
    sizes, gin, q_ref, w_hbm, mod_ref, step_ref, win_ref, out_ref,
    grid, bias, attn, w_ref, total, y_out, y_in,
    halo_send, halo_recv, attn_send, attn_recv, y_send, y_recv, local_sem,
):
    n_frame, n_row, n_col = sizes
    slots = grid.shape[0]
    groups = gin.shape[4] // (2 * HEAD_DIM)
    tokens = q_ref.shape[0]
    count = tokens // gin.shape[0]
    own_frames, own_rps, own_cps = gin.shape[:3]
    me_f = lax.axis_index("frame")
    me_r = lax.axis_index("row")
    me_c = lax.axis_index("fsdp")

    w_copy = pltpu.make_async_copy(w_hbm, w_ref, local_sem.at[0])
    w_copy.start()
    own_copy = pltpu.make_async_copy(
        gin, grid.at[pl.ds(0, own_frames), pl.ds(0, own_rps), pl.ds(0, own_cps)], local_sem.at[1]
    )
    own_copy.start()

    barrier = pltpu.get_barrier_semaphore()

    def neighbours(axis, me, count):
        return ((axis, me + 1, me < count - 1), (axis, me - 1, me > 0))

    near = neighbours("frame", me_f, n_frame) + neighbours("row", me_r, n_row)
    for axis, other, there in near:
        @pl.when(there)
        def _():
            pl.semaphore_signal(barrier, inc=1, device_id={axis: other}, device_id_type=MESH)

    def greet(k, carry):
        peer = lax.rem(me_c + k, n_col)
        pl.semaphore_signal(barrier, inc=1, device_id={"fsdp": peer}, device_id_type=MESH)
        return carry

    lax.fori_loop(1, n_col, greet, 0)
    greetings = n_col - 1
    for _, _, there in near:
        greetings += there.astype(jnp.int32)
    pl.semaphore_wait(barrier, greetings)

    def copy(src, dst, index, axis, other):
        return pltpu.make_async_remote_copy(
            src_ref=src, dst_ref=dst, send_sem=halo_send.at[index], recv_sem=halo_recv.at[index],
            device_id={axis: other}, device_id_type=MESH,
        )

    own_f = pl.ds(0, own_frames)
    halo_f = pl.ds(own_frames, slots - own_frames)
    own_r = pl.ds(0, own_rps)
    halo_r = pl.ds(own_rps, 2)
    own_c = pl.ds(0, own_cps)
    below, above = own_rps, own_rps + 1
    left, right = own_cps, own_cps + 1
    low_slot, high_slot = own_frames, slots - 1
    steps = {}

    def add(name, axis, me, count, index, up, down):
        steps[name] = (
            (copy(up[0], up[1], index, axis, me + 1), me < count - 1, me > 0),
            (copy(down[0], down[1], index + 1, axis, me - 1), me > 0, me < count - 1),
        )

    every = slice(None)
    all_r = pl.ds(0, own_rps + 2)
    for part, (low, high) in enumerate(CHUNKS):
        base = 12 * part
        tail = (every, pl.ds(low * 2 * HEAD_DIM, (high - low) * 2 * HEAD_DIM))

        def own(*place):
            return gin.at[place + tail]

        def held(*place):
            return grid.at[place + tail]

        add(("f", part), "frame", me_f, n_frame, base,
            (own(own_frames - 1, every, every), held(low_slot, own_r, own_c)),
            (own(0, every, every), held(high_slot, own_r, own_c)))
        add(("r1", part), "row", me_r, n_row, base + 2,
            (own(every, own_rps - 1, every), held(own_f, below, own_c)),
            (own(every, 0, every), held(own_f, above, own_c)))
        add(("r2", part), "row", me_r, n_row, base + 4,
            (held(halo_f, own_rps - 1, own_c), held(halo_f, below, own_c)),
            (held(halo_f, 0, own_c), held(halo_f, above, own_c)))
        add(("c1", part), "fsdp", me_c, n_col, base + 6,
            (own(every, every, own_cps - 1), held(own_f, own_r, left)),
            (own(every, every, 0), held(own_f, own_r, right)))
        add(("c2", part), "fsdp", me_c, n_col, base + 8,
            (held(own_f, halo_r, own_cps - 1), held(own_f, halo_r, left)),
            (held(own_f, halo_r, 0), held(own_f, halo_r, right)))
        add(("c3", part), "fsdp", me_c, n_col, base + 10,
            (held(halo_f, all_r, own_cps - 1), held(halo_f, all_r, left)),
            (held(halo_f, all_r, 0), held(halo_f, all_r, right)))

    def start(name, part):
        for step, sends, _ in steps[name, part]:
            @pl.when(sends)
            def _():
                step.start()

    def arrive(name, part):
        for step, _, receives in steps[name, part]:
            @pl.when(receives)
            def _():
                step.wait_recv()

    start("f", 0)
    start("r1", 0)
    start("c1", 0)

    for edge, at_edge in (
        ((slice(None), below), me_r == 0),
        ((slice(None), above), me_r == n_row - 1),
    ):
        @pl.when(at_edge)
        def _():
            for slot in range(slots):
                grid[(slot, edge[1], pl.ds(0, own_cps))] = jnp.zeros(
                    (own_cps,) + grid.shape[3:], grid.dtype)
    for place, at_edge in ((left, me_c == 0), (right, me_c == n_col - 1)):
        @pl.when(at_edge)
        def _():
            for slot in range(slots):
                grid[slot, :, place] = jnp.zeros((grid.shape[1],) + grid.shape[3:], grid.dtype)
    if slots - own_frames == 2:
        for place, at_edge in ((low_slot, me_f == 0), (high_slot, me_f == n_frame - 1)):
            @pl.when(at_edge)
            def _():
                for pair in range(own_rps):
                    grid[place, pair, pl.ds(0, own_cps)] = jnp.zeros(
                        (own_cps,) + grid.shape[3:], grid.dtype)

    arrive("r1", 0)
    start("c2", 0)

    keys = bias.shape[2]
    shape = (tokens, keys)
    rows, columns = 2 * own_rps, 2 * own_cps
    at = lax.broadcasted_iota(jnp.int32, shape, 0)
    q_f = jnp.zeros(shape, jnp.int32)
    for f in range(1, own_frames):
        q_f += (at >= f * rows * columns).astype(jnp.int32)
    at = at - q_f * (rows * columns)
    q_r = jnp.zeros(shape, jnp.int32)
    for r in range(1, rows):
        q_r += (at >= r * columns).astype(jnp.int32)
    q_c = at - q_r * columns
    lane = lax.broadcasted_iota(jnp.int32, shape, 1)
    slot = lane >> 7
    pair_r = (lane >> 5) & 3
    pair_c = (lane >> 2) & 7
    if slots - own_frames == 1:
        halo_at = jnp.where(me_f == 0, own_frames, -1)
        k_f = jnp.where(slot == own_frames, halo_at, slot)
    else:
        k_f = jnp.where(slot == low_slot, -1, slot)
        k_f = jnp.where(slot == high_slot, own_frames, k_f)
    pair_r = jnp.where(pair_r == below, -1, jnp.where(pair_r == above, own_rps, pair_r))
    pair_c = jnp.where(pair_c == left, -1, jnp.where(pair_c == right, own_cps, pair_c))
    k_r = 2 * pair_r + ((lane >> 1) & 1)
    k_c = 2 * pair_c + (lane & 1)
    g_f = k_f + me_f * own_frames
    g_r = k_r + me_r * rows
    g_c = k_c + me_c * columns
    inside = (
        (g_f >= 0) & (g_f < n_frame * own_frames)
        & (g_r >= 0) & (g_r < n_row * rows)
        & (g_c >= 0) & (g_c < n_col * columns)
    )
    d_f = jnp.where(inside, jnp.abs(k_f - q_f), 1000)
    d_r = jnp.abs(k_r - q_r)
    d_c = jnp.abs(k_c - q_c)

    def make_bias(head, carry):
        ok = (d_f <= win_ref[0, head]) & (d_r <= win_ref[1, head]) & (d_c <= win_ref[2, head])
        bias[head] = jnp.where(ok, jnp.float32(0), jnp.float32(-1e30))
        return carry

    lax.fori_loop(0, QUARTERS * groups, make_bias, 0)

    own_copy.wait()
    arrive("c1", 0)
    arrive("c2", 0)

    apart = n_frame == 2

    def frame_at(turn):
        if not apart:
            return turn
        return me_f if turn == 0 else own_frames - 1 - me_f

    def frame_rows(turn):
        return pl.ds(pl.multiple_of(frame_at(turn) * count, 16), count)

    def relay(number):
        if number == 0:
            arrive("f", 0)
            start("r2", 0)
        else:
            arrive("r2", 0)
            start("c3", 0)

    if not apart:
        relay(0)
        relay(1)
        arrive("c3", 0)

    pairs = grid.shape[1] * grid.shape[2]
    scale = 1.0 / math.sqrt(HEAD_DIM)

    def block_copy(j, origin, way):
        other = me_c + 1 - 2 * way
        return pltpu.make_async_remote_copy(
            src_ref=attn.at[j, origin], dst_ref=attn.at[j, origin],
            send_sem=attn_send.at[j, way, origin], recv_sem=attn_recv.at[j, origin],
            device_id={"fsdp": other}, device_id_type=MESH,
        )

    def wait_block(j, origin):
        block_copy(j, origin, 0).wait_recv()

    passes = (me_c < n_col - 1, me_c > 0)

    def attend(turn):
        used = own_frames if apart and turn == 0 else slots
        for j in range(groups):
            if apart and turn == 0 and j in (1, 3):
                relay(j // 2)
            attend_group(turn, j, used)

    def attend_group(turn, j, used):
        granules = used * pairs
        length = granules * 4
        rows = frame_rows(turn)
        lanes = pl.ds(j * 2 * HEAD_DIM, 2 * HEAD_DIM)
        block = grid[pl.ds(0, used), :, :, :, lanes].astype(jnp.float32)
        block = block.reshape(granules // 2, 2, 2, 8, 2 * HEAD_DIM)
        first, second = block[:, 0], block[:, 1]
        turned_first = pltpu.roll(block[:, 0].reshape(-1, 8, 2 * HEAD_DIM), 4, 1).reshape(first.shape)
        turned_second = pltpu.roll(block[:, 1].reshape(-1, 8, 2 * HEAD_DIM), 4, 1).reshape(first.shape)
        upper = lax.broadcasted_iota(jnp.int32, first.shape, 2) < 4
        even = jnp.where(upper, first, turned_second)
        odd = jnp.where(upper, turned_first, second)
        for quarter in range(QUARTERS):
            head = quarter * groups + j
            dense = (even, odd)[quarter % 2][:, quarter // 2].reshape(length, 2 * HEAD_DIM)
            dense = dense.astype(jnp.bfloat16)
            query = q_ref[rows, pl.ds(head * HEAD_DIM, HEAD_DIM)]
            scores = lax.dot_general(
                query, dense[:, :HEAD_DIM], (((1,), (1,)), ((), ())),
                preferred_element_type=jnp.float32,
            )
            scores = scores * scale + bias[head, rows, pl.ds(0, length)]
            exponent = jnp.exp(scores - jnp.max(scores, axis=-1, keepdims=True))
            denominator = jnp.sum(exponent, axis=-1, keepdims=True)
            weights = (exponent * (1.0 / denominator)).astype(jnp.bfloat16)
            result = jnp.dot(weights, dense[:, HEAD_DIM:], preferred_element_type=jnp.float32)
            attn[turn * groups + j, me_c, :, pl.ds(quarter * HEAD_DIM, HEAD_DIM)] = result.astype(jnp.bfloat16)

        for way in range(2):
            @pl.when(passes[way])
            def _():
                block_copy(turn * groups + j, me_c, way).start()

    def y_copy(turn, peer):
        return pltpu.make_async_remote_copy(
            src_ref=y_out.at[turn, peer], dst_ref=y_in.at[turn, me_c],
            send_sem=y_send.at[turn, peer], recv_sem=y_recv.at[turn, me_c],
            device_id={"fsdp": peer}, device_id_type=MESH,
        )

    def product(turn, j, origin):
        weight = jnp.concatenate(
            [w_ref[pl.ds((quarter * groups + j) * HEAD_DIM, HEAD_DIM), :]
             for quarter in range(QUARTERS)], axis=0)
        return jnp.dot(attn[turn * groups + j, origin], weight, preferred_element_type=jnp.float32)

    def distance(turn, d, carry):
        origins = (me_c - d, me_c + d)
        there = (origins[0] >= 0, origins[1] < n_col)
        for j in range(groups):
            for way in range(2):
                @pl.when(there[way])
                def _():
                    wait_block(turn * groups + j, origins[way])

                    @pl.when(passes[way])
                    def _():
                        block_copy(turn * groups + j, origins[way], way).start()
            for way in range(2):
                @pl.when(there[way])
                def _():
                    part = product(turn, j, origins[way])
                    if j > 0:
                        part = total[way] + part
                    if j < groups - 1:
                        total[way] = part
                    else:
                        y_out[turn, origins[way]] = (part * gate).astype(jnp.bfloat16)
                        y_copy(turn, origins[way]).start()
        return carry

    width = w_ref.shape[1]
    table_row = mod_ref[pl.ds(step_ref[0], 1), :]
    gate = table_row[:, :width]
    for place in range(1, n_col):
        gate = jnp.where(me_c == place, table_row[:, place * width:(place + 1) * width], gate)
    turns = own_frames
    attend(0)
    w_copy.wait()
    distance(0, 1, 0)
    if apart:
        arrive("c3", 0)
    for turn in range(1, turns):
        attend(turn)
    for turn in range(turns):
        lax.fori_loop(2 if turn == 0 else 1, n_col, functools.partial(distance, turn), 0)
    for turn in range(turns):
        mine = product(turn, 0, me_c)
        for j in range(1, groups):
            mine += product(turn, j, me_c)
        y_in[turn, me_c] = (mine * gate).astype(jnp.bfloat16)

    for turn in range(turns):
        def y_wait(k, carry):
            peer = lax.rem(me_c + k, n_col)
            pltpu.make_async_remote_copy(
                src_ref=y_out.at[turn, peer], dst_ref=y_in.at[turn, peer],
                send_sem=y_send.at[turn, peer], recv_sem=y_recv.at[turn, peer],
                device_id={"fsdp": peer}, device_id_type=MESH,
            ).wait_recv()
            return carry

        lax.fori_loop(1, n_col, y_wait, 0)
        for place in range(n_col):
            out_ref[frame_rows(turn), place * width:(place + 1) * width] = y_in[turn, place]

    for name in steps:
        for step, sends, _ in steps[name]:
            @pl.when(sends)
            def _():
                step.wait_send()
    for number in range(turns * groups):
        for way in range(2):
            def sent(d, carry):
                origin = me_c - d + 2 * d * way

                @pl.when(passes[way] & (origin >= 0) & (origin < n_col))
                def _():
                    block_copy(number, origin, way).wait_send()
                return carry

            lax.fori_loop(0, n_col, sent, 0)
    for turn in range(turns):
        def y_sent(k, carry):
            y_copy(turn, lax.rem(me_c + k, n_col)).wait_send()
            return carry

        lax.fori_loop(1, n_col, y_sent, 0)


def body(query, key_value, out_weight, mod_table, step, window):
    frames, rows, columns, features = query.shape
    heads = features // HEAD_DIM
    groups = heads // QUARTERS
    tokens = frames * rows * columns
    width = out_weight.shape[1]
    n_frame, n_row, n_col = (lax.axis_size(a) for a in ("frame", "row", "fsdp"))
    slots = frames + (1 if n_frame == 2 else 2)
    pairs = key_value.reshape(
        2, frames, rows // 2, 2, columns // 2, 2, QUARTERS, groups, HEAD_DIM)
    granules = pairs.transpose(1, 2, 4, 6, 3, 5, 7, 0, 8).reshape(
        frames, rows // 2, columns // 2, QUARTERS * 4, groups * 2 * HEAD_DIM)
    block = (slots, rows // 2 + 2, columns // 2 + 2)
    keys = block[0] * block[1] * block[2] * 4
    vmem = pl.BlockSpec(memory_space=pltpu.VMEM)
    out = pl.pallas_call(
        functools.partial(kernel, (n_frame, n_row, n_col)),
        out_shape=jax.ShapeDtypeStruct((tokens, n_col * width), jnp.bfloat16),
        in_specs=[vmem, vmem, pl.BlockSpec(memory_space=pl.ANY), vmem,
                  pl.BlockSpec(memory_space=pltpu.SMEM), pl.BlockSpec(memory_space=pltpu.SMEM)],
        out_specs=vmem,
        scratch_shapes=[
            pltpu.VMEM(block + granules.shape[3:], jnp.bfloat16),
            pltpu.VMEM((heads, tokens, keys), jnp.float32),
            pltpu.VMEM((frames * groups, n_col, tokens // frames, QUARTERS * HEAD_DIM), jnp.bfloat16),
            pltpu.VMEM(out_weight.shape, jnp.bfloat16),
            pltpu.VMEM((2, tokens // frames, width), jnp.float32),
            pltpu.VMEM((frames, n_col, tokens // frames, width), jnp.bfloat16),
            pltpu.VMEM((frames, n_col, tokens // frames, width), jnp.bfloat16),
            pltpu.SemaphoreType.DMA((12 * len(CHUNKS),)),
            pltpu.SemaphoreType.DMA((12 * len(CHUNKS),)),
            pltpu.SemaphoreType.DMA((frames * groups, 2, n_col)),
            pltpu.SemaphoreType.DMA((frames * groups, n_col)),
            pltpu.SemaphoreType.DMA((frames, n_col)),
            pltpu.SemaphoreType.DMA((frames, n_col)),
            pltpu.SemaphoreType.DMA((2,)),
        ],
        compiler_params=pltpu.CompilerParams(
            collective_id=0, has_side_effects=True, vmem_limit_bytes=40 * 1024 * 1024),
    )(granules, query.reshape(tokens, features), out_weight, mod_table, step, window.T)
    return out.reshape(frames, rows, columns, -1)


def solution(mesh):
    return jax.shard_map(
        body,
        mesh=mesh,
        in_specs=(
            P("frame", "row", "fsdp", None),
            P(None, "frame", "row", "fsdp", None),
            P(None, "fsdp"),
            P(),
            P(),
            P(),
        ),
        out_specs=P("frame", "row", "fsdp", None),
        check_vma=False,
    )
```
